128 devices in a mesh: seq: 32 (over y, x, core), seqs: 4 (over z).
Axes of the slice: x: 4, y: 4, z: 4, core: 2. Of those that a mesh axis runs over, the one named last changes fastest.
Arguments:
- queries: float32 [524288, 2, 128], P(('seqs', 'seq')), parts along dimension 0, may hold values from -0.09375 to 0.09375
- key_vectors: float32 [524288, 2, 128], P(('seqs', 'seq')), parts along dimension 0, may hold values from -0.09375 to 0.09375
- value_vectors: float32 [524288, 2, 128], P(('seqs', 'seq')), parts along dimension 0, may hold values from -0.09375 to 0.09375
- grad_output: float32 [524288, 2, 128], P(('seqs', 'seq')), parts along dimension 0, may hold values from -6 to 6
Outputs:
- grad_queries: float32 [524288, 2, 128], P(('seqs', 'seq')), parts along dimension 0
- grad_keys: float32 [524288, 2, 128], P(('seqs', 'seq')), parts along dimension 0
- grad_values: float32 [524288, 2, 128], P(('seqs', 'seq')), parts along dimension 0
The draws below stay inside these ranges and needn't reach their ends.
There are 4 independent parts, one for each index of `seqs`. The reference program is written for one: setup_inputs(seed, part) draws one part's arguments, and reference() takes and returns one part's arrays. A program takes and returns all parts, laid end to end along the dimension named above; each array names one. Nothing has to cross between parts.
All inputs are finite; a program needn't handle non-finite values.
Results may differ from the reference program's by a relative error of at most 0.0001.
Values sent between devices are 32-bit elements; how exact they have to be, the bound alone decides.
No kernel may reach another device: no remote copies, remote signals or barrier semaphores. Data moves between devices by JAX's collectives and lax.ppermute only.
A program may use at most 192 MiB of HBM per device.

```python
import jax
import jax.numpy as jnp
from jax import lax

HEAD = 128
HEADS = 2
BLK = 512
TOKENS = 131072


def block_levels(stream_key, extent, cuts, low, top_value):
    def one(axis_at, shards_of):
        heights = jax.random.uniform(jax.random.fold_in(jax.random.fold_in(stream_key, 6), axis_at), (shards_of,), jnp.float32, low / len(cuts), top_value / len(cuts))
        return jnp.repeat(jnp.exp(heights), extent[axis_at] // shards_of).reshape((-1,) + (1,) * (len(extent) - axis_at - 1))

    factor_of = one(*cuts[0])
    for cut in cuts[1:]:
        factor_of = factor_of * one(*cut)
    return factor_of


def bell_draw(stream_key, dims, scale, most, shards=(), dtype=jnp.bfloat16):
    result = jax.random.normal(stream_key, dims, jnp.float32) * scale
    if len(shards) > 0:
        result = block_levels(stream_key, dims, shards, -0.22, 0.18) * result
    return jnp.clip(result, min=-most, max=most).astype(dtype)


def setup_inputs(seed: int = 0, part: int = 0) -> dict:
    seeds = jax.random.split(jax.random.key(seed), 5)
    part_splits = jax.random.split(jax.random.fold_in(seeds[4], part), 5)
    return {
        "queries": bell_draw(part_splits[0], (TOKENS, HEADS, HEAD), (1.0 / (HEAD * TOKENS) ** 0.25), 0.09375, ((0, 32),), jnp.float32),
        "key_vectors": bell_draw(part_splits[1], (TOKENS, HEADS, HEAD), (1.0 / (HEAD * TOKENS) ** 0.25), 0.09375, ((0, 32),), jnp.float32),
        "value_vectors": bell_draw(part_splits[2], (TOKENS, HEADS, HEAD), (1.0 / (HEAD * TOKENS) ** 0.25), 0.09375, ((0, 32),), jnp.float32),
        "grad_output": bell_draw(part_splits[3], (TOKENS, HEADS, HEAD), 1.0, 6.0, ((0, 32),), jnp.float32),
    }


HIGH = lax.Precision.HIGHEST


def reference(queries, key_vectors, value_vectors, grad_output):
    count = queries.shape[0] // BLK
    shape = (count, BLK, HEADS, HEAD)
    qb = queries.reshape(shape)
    kb = key_vectors.reshape(shape)
    vb = value_vectors.reshape(shape)
    gb = grad_output.reshape(shape)
    block_state = jnp.einsum('nthe,nthf->nhef', kb, vb, precision=HIGH)
    block_grad = jnp.einsum('nthe,nthf->nhef', qb, gb, precision=HIGH)
    prefix_state = jnp.cumsum(block_state, axis=0) - block_state
    suffix_grad = jnp.cumsum(block_grad[::-1], axis=0)[::-1] - block_grad
    causal = jnp.tril(jnp.ones((BLK, BLK), jnp.float32))

    def one_block(items):
        qx, kx, vx, gx, pre, suf = items
        scores = jnp.einsum('the,she->hts', qx, kx, precision=HIGH) * causal
        grad_scores = jnp.einsum('the,she->hts', gx, vx, precision=HIGH) * causal
        dquery = jnp.einsum('hts,she->the', grad_scores, kx, precision=HIGH) + jnp.einsum('thf,hef->the', gx, pre, precision=HIGH)
        dkey = jnp.einsum('hts,the->she', grad_scores, qx, precision=HIGH) + jnp.einsum('thf,hef->the', vx, suf, precision=HIGH)
        dvalue = jnp.einsum('hts,thf->shf', scores, gx, precision=HIGH) + jnp.einsum('the,hef->thf', kx, suf, precision=HIGH)
        return dquery, dkey, dvalue

    dquery, dkey, dvalue = lax.map(one_block, (qb, kb, vb, gb, prefix_state, suffix_grad))
    full = queries.shape
    return dquery.reshape(full), dkey.reshape(full), dvalue.reshape(full)
```

```python
import functools

import jax
import jax.numpy as jnp
from jax import lax
from jax.experimental import pallas as pl
from jax.experimental.pallas import tpu as pltpu
from jax.sharding import PartitionSpec as P

HEAD = 128
HEADS = 2
CHUNK = 128
SLICES = 4

BF16 = jnp.bfloat16
F32 = jnp.float32
NAT = (((1,), (0,)), ((), ()))
ROWS = (((1,), (1,)), ((), ()))
COLS = (((0,), (0,)), ((), ()))
MIB = 1024 * 1024


def mm(a, b, dims=NAT):
    return lax.dot_general(a, b, dims, preferred_element_type=F32)


def parts(x):
    hi = x.astype(BF16)
    lo = (x - hi.astype(F32)).astype(BF16)
    return hi, lo


def pair(x):
    return jnp.concatenate(parts(x), axis=1)


def stacked(xx):
    hi, lo = xx[:, :HEAD], xx[:, HEAD:]
    top = jnp.concatenate([hi, hi], axis=1)
    low = jnp.concatenate([lo, lo], axis=1)
    return jnp.concatenate([top, low], axis=0)


def halves(x):
    return x[:, :HEAD] + x[:, HEAD:]


def quads(x):
    return x[:CHUNK, :HEAD] + x[:CHUNK, HEAD:] + x[CHUNK:, :HEAD]


def states_kernel(tile, q, k, v, g, qs, ks, vs, gs, pt, sg, sgt, own_p, own_s, kb, vb, qb, gb, sems):
    tokens = q.shape[0] // HEADS
    steps = tokens // tile
    rows = tile * HEADS

    def fetch(step, slot):
        back = steps - 1 - step
        out = []
        for j, (src, dst, at) in enumerate(((k, kb, step), (v, vb, step), (q, qb, back), (g, gb, back))):
            out.append(pltpu.make_async_copy(src.at[pl.ds(at * rows, rows)], dst.at[slot], sems.at[j, slot]))
        return out

    for c in fetch(0, 0):
        c.start()
    own_p[...] = jnp.zeros_like(own_p)
    own_s[...] = jnp.zeros_like(own_s)
    per = tile // CHUNK

    def body(step, carry):
        slot = lax.rem(step, 2)

        @pl.when(step + 1 < steps)
        def _():
            for c in fetch(step + 1, 1 - slot):
                c.start()

        for c in fetch(step, slot):
            c.wait()
        back = steps - 1 - step
        for c in range(per):
            r = per - 1 - c
            for h in range(HEADS):
                tok = pl.ds(pl.multiple_of(step * tile + c * CHUNK, CHUNK), CHUNK)
                inside = pl.ds(c * CHUNK * HEADS + h, CHUNK, HEADS)
                kk = pair(kb[slot, inside, :])
                vv = pair(vb[slot, inside, :])
                ks[h, tok, :] = kk
                vs[h, tok, :] = vv
                p = own_p[h]
                pt[step * per + c, h] = pair(p)
                own_p[h] = p + quads(mm(vv, kk, COLS))

                tok = pl.ds(pl.multiple_of(back * tile + r * CHUNK, CHUNK), CHUNK)
                inside = pl.ds(r * CHUNK * HEADS + h, CHUNK, HEADS)
                qq = pair(qb[slot, inside, :])
                gg = pair(gb[slot, inside, :])
                qs[h, tok, :] = qq
                gs[h, tok, :] = gg
                s = own_s[h]
                sg[back * per + r, h] = pair(s)
                sgt[back * per + r, h] = pair(s.T)
                own_s[h] = s + quads(mm(qq, gg, COLS))
        return carry

    lax.fori_loop(0, steps, body, 0)


def inside_kernel(first, count, unroll, qs, ks, vs, gs, pt, sg, sgt, dq, dk, dv):
    at_row = lax.broadcasted_iota(jnp.int32, (CHUNK, CHUNK), 0)
    at_col = lax.broadcasted_iota(jnp.int32, (CHUNK, CHUNK), 1)
    upper = at_row <= at_col
    lower = at_row >= at_col

    def one(n, h):
        tok = pl.ds(pl.multiple_of((first + n) * CHUNK, CHUNK), CHUNK)
        out = pl.ds(pl.multiple_of(n * CHUNK, CHUNK), CHUNK)
        qq, kk, vv, gg = (x[h, tok, :] for x in (qs, ks, vs, gs))

        def finish(score, keep, left, right, state):
            hi, lo = parts(jnp.where(keep, halves(score), 0.0))
            top = jnp.concatenate([hi, left[:, :HEAD]], axis=1)
            low = jnp.concatenate([lo, left[:, HEAD:]], axis=1)
            lhs = jnp.concatenate([top, low], axis=0)
            return quads(mm(lhs, jnp.concatenate([right, state], axis=0)))

        dq[h, out, :] = finish(mm(gg, stacked(vv), ROWS), lower, gg, kk, pt[first + n, h])
        dk[h, out, :] = finish(mm(vv, stacked(gg), ROWS), upper, vv, qq, sgt[first + n, h])
        dv[h, out, :] = finish(mm(kk, stacked(qq), ROWS), upper, kk, gg, sg[first + n, h])

    def body(i, carry):
        for u in range(unroll):
            for h in range(HEADS):
                one(i * unroll + u, h)
        return carry

    lax.fori_loop(0, count // unroll, body, 0)


def outside_kernel(tile, slices, ks, vs, gs, before, after, *rest):
    partial = rest[: 3 * slices]
    outs = rest[3 * slices : 3 * slices + 3]
    ob, sems = rest[3 * slices + 3 :]
    tokens = ks.shape[1]
    steps = tokens // tile
    rows = tile * HEADS
    span = tokens // slices
    weights = []
    for h in range(HEADS):
        b = pair(before[h])
        a = pair(after[h])
        weights.append((jnp.concatenate([b, b], axis=0), stacked(a), jnp.concatenate([a, a], axis=0)))

    def send(j, step, slot):
        return pltpu.make_async_copy(ob.at[j, slot], outs[j].at[pl.ds(step * rows, rows)], sems.at[j, slot])

    for step in range(steps):
        slot = step % 2
        base = step * tile
        part, off = base // span, base % span
        for j, (src, dims) in enumerate(((gs, NAT), (vs, ROWS), (ks, NAT))):
            if step >= 2:
                send(j, step - 2, slot).wait()
            for h in range(HEADS):
                x = halves(mm(src[h, base : base + tile, :], weights[h][j], dims))
                ob[j, slot, pl.ds(h, tile, HEADS), :] = x + partial[part * 3 + j][h, off : off + tile, :]
            send(j, step, slot).start()
    for step in range(max(steps - 2, 0), steps):
        for j in range(3):
            send(j, step, step % 2).wait()


VM = pl.BlockSpec(memory_space=pltpu.VMEM)
ANY = pl.BlockSpec(memory_space=pl.ANY)


def vmem(*arrays):
    return [pltpu.with_memory_space_constraint(a, pltpu.VMEM) for a in arrays]


def body(shape, queries, key_vectors, value_vectors, grad_output):
    tokens = queries.shape[0]
    chunks = tokens // CHUNK
    flat = [x.reshape(tokens * HEADS, HEAD) for x in (queries, key_vectors, value_vectors, grad_output)]

    tile = 512
    split_shape = pltpu.VMEM((HEADS, tokens, 2 * HEAD), BF16)
    state_shape = pltpu.VMEM((chunks, HEADS, HEAD, 2 * HEAD), BF16)
    own_shape = pltpu.VMEM((HEADS, HEAD, HEAD), F32)
    *split, pt, sg, sgt, own_p, own_s = pl.pallas_call(
        functools.partial(states_kernel, tile),
        out_shape=[split_shape] * 4 + [state_shape] * 3 + [own_shape] * 2,
        in_specs=[ANY] * 4,
        out_specs=[VM] * 9,
        scratch_shapes=[pltpu.VMEM((2, tile * HEADS, HEAD), F32)] * 4 + [pltpu.SemaphoreType.DMA((4, 2))],
        compiler_params=pltpu.CompilerParams(vmem_limit_bytes=8 * MIB),
        cost_estimate=pl.CostEstimate(flops=10**9, bytes_accessed=16 * MIB, transcendentals=0),
        name="states",
    )(*flat)

    core = lax.axis_index("seq") % 2
    mine = jnp.where(core == 0, own_p, own_s)
    other = jnp.where(core == 0, own_s, own_p)
    devices = lax.axis_size("seq")
    here = lax.axis_index("seq")
    sibling = [(i, i ^ 1) for i in range(devices)]
    total = mine + lax.ppermute(other, "seq", sibling)
    entered = jnp.zeros_like(total)

    count = chunks // SLICES
    partial = []

    def inside(at, after):
        fed = vmem(*split, pt, sg, sgt)
        return pl.pallas_call(
            functools.partial(inside_kernel, at * count, count, 1),
            out_shape=[pltpu.VMEM((HEADS, tokens // SLICES, HEAD), F32)] * 3,
            in_specs=[VM] * 7,
            out_specs=[VM] * 3,
            compiler_params=pltpu.CompilerParams(vmem_limit_bytes=8 * MIB),
            cost_estimate=pl.CostEstimate(flops=3 * 10**9, bytes_accessed=MIB, transcendentals=0),
            name="inside" + str(at),
        )(*fed)

    step = 2
    at = 0
    while step < devices:
        got = lax.ppermute(total, "seq", [(i, i ^ step) for i in range(devices)])
        partial += inside(at, None)
        at += 1
        partner_first = ((here & step) != 0) == (core == 0)
        entered = entered + jnp.where(partner_first, got, 0.0)
        total = total + got
        step *= 2
    while at < SLICES:
        partial += inside(at, None)
        at += 1
    got = lax.ppermute(entered + mine, "seq", sibling)
    before = jnp.where(core == 0, entered, got)
    after = jnp.where(core == 0, got, entered)

    tile = 256
    out = pl.pallas_call(
        functools.partial(outside_kernel, tile, SLICES),
        out_shape=[jax.ShapeDtypeStruct((tokens * HEADS, HEAD), F32)] * 3,
        in_specs=[VM] * (5 + 3 * SLICES),
        out_specs=[ANY] * 3,
        scratch_shapes=[pltpu.VMEM((3, 2, tile * HEADS, HEAD), F32), pltpu.SemaphoreType.DMA((3, 2))],
        compiler_params=pltpu.CompilerParams(vmem_limit_bytes=8 * MIB),
        cost_estimate=pl.CostEstimate(flops=10**9, bytes_accessed=12 * MIB, transcendentals=0),
        name="outside",
    )(*vmem(split[1], split[2], split[3], before, after, *partial))
    return tuple(x.reshape(queries.shape) for x in out)


def solution(mesh):
    spec = P(("seqs", "seq"), None, None)
    return jax.shard_map(
        functools.partial(body, dict(mesh.shape)),
        mesh=mesh,
        in_specs=(spec,) * 4,
        out_specs=(spec,) * 3,
        check_vma=False,
    )
```

```python
import functools

import jax
import jax.numpy as jnp
from jax import lax
from jax.experimental import pallas as pl
from jax.experimental.pallas import tpu as pltpu
from jax.sharding import PartitionSpec as P

HEAD = 128
HEADS = 2
CHUNK = 128
CUTS = (3, 7, 7, 6, 6, 3)
SLICES = len(CUTS)

BF16 = jnp.bfloat16
F32 = jnp.float32
NAT = (((1,), (0,)), ((), ()))
ROWS = (((1,), (1,)), ((), ()))
COLS = (((0,), (0,)), ((), ()))
MIB = 1024 * 1024


def cut_sizes(chunks):
    edges = [sum(CUTS[:i]) * chunks // sum(CUTS) for i in range(SLICES + 1)]
    return [b - a for a, b in zip(edges, edges[1:])], edges[:-1]


def mm(a, b, dims=NAT):
    return lax.dot_general(a, b, dims, preferred_element_type=F32)


def parts(x):
    hi = x.astype(BF16)
    lo = (x - hi.astype(F32)).astype(BF16)
    return hi, lo


def pair(x):
    return jnp.concatenate(parts(x), axis=1)


def stacked(xx):
    hi, lo = xx[:, :HEAD], xx[:, HEAD:]
    top = jnp.concatenate([hi, hi], axis=1)
    low = jnp.concatenate([lo, lo], axis=1)
    return jnp.concatenate([top, low], axis=0)


def halves(x):
    return x[:, :HEAD] + x[:, HEAD:]


def twice(xx):
    return jnp.concatenate([xx, xx], axis=0)


def gram(hi, lo, yy):
    return halves(mm(jnp.concatenate([hi, lo], axis=0), twice(yy), COLS))


def states_kernel(tile, q, k, v, g, ks, vs, gs, mine, other, *rest):
    qs, pt, sg, sgt = (rest[j * SLICES : (j + 1) * SLICES] for j in range(4))
    kb, vb, qb, gb, own, sems = rest[4 * SLICES :]
    tokens = q.shape[0] // HEADS
    steps = tokens // tile
    rows = tile * HEADS
    per = tile // CHUNK
    place = [(i, n) for i, size in enumerate(cut_sizes(tokens // CHUNK)[0]) for n in range(size)]

    def fetch(step):
        back = steps - 1 - step
        return [
            pltpu.make_async_copy(src.at[pl.ds(at * rows, rows)], dst.at[step], sems.at[j, step])
            for j, (src, dst, at) in enumerate(((k, kb, step), (v, vb, step), (q, qb, back), (g, gb, back)))
        ]

    for step in range(steps):
        for c in fetch(step):
            c.start()
    core = lax.rem(lax.axis_index("seq"), 2)
    own[...] = jnp.zeros_like(own)
    for step in range(steps):
        for c in fetch(step):
            c.wait()
        back = steps - 1 - step
        for h in range(HEADS):
            p, s = own[0, h], own[1, h]
            for c in range(per):
                n = step * per + c
                tok = slice(n * CHUNK, (n + 1) * CHUNK)
                inside = pl.ds(c * CHUNK * HEADS + h, CHUNK, HEADS)
                kk = pair(kb[step, inside, :])
                vhi, vlo = parts(vb[step, inside, :])
                ks[h, tok, :] = kk
                vs[h, tok, :] = jnp.concatenate([vhi, vlo], axis=1)
                i, m = place[n]
                pt[i][m, h] = pair(p)
                p = p + gram(vhi, vlo, kk)

                r = per - 1 - c
                n = back * per + r
                tok = slice(n * CHUNK, (n + 1) * CHUNK)
                inside = pl.ds(r * CHUNK * HEADS + h, CHUNK, HEADS)
                qhi, qlo = parts(qb[step, inside, :])
                gg = pair(gb[step, inside, :])
                i, m = place[n]
                qs[i][h, m * CHUNK : (m + 1) * CHUNK, :] = jnp.concatenate([qhi, qlo], axis=1)
                gs[h, tok, :] = gg
                shi, slo = parts(s)
                sg[i][m, h] = jnp.concatenate([shi, slo], axis=1)
                sgt[i][m, h] = jnp.concatenate([shi.T, slo.T], axis=1)
                s = s + gram(qhi, qlo, gg)
            own[0, h] = p
            own[1, h] = s
    mine[...] = own[core]
    other[...] = own[1 - core]


def first_kernel(mine, got, order, total):
    total[...] = mine[...] + got[...]


def scan_kernel(step, first, last, mine, total, got, order, *rest):
    *entered, new_total, new_entered = rest
    here = lax.axis_index("seq")
    core = lax.rem(here, 2)
    bit = lax.rem(lax.div(here, step), 2)
    take = jnp.where(bit + core == 1, 1.0, 0.0)
    new = got[...] * take
    if not first:
        new += entered[0][...]
    new_entered[...] = new
    new_total[...] = new + mine[...] if last else total[...] + got[...]


def inside_kernel(first, count, qs, ks, vs, gs, pt, sg, sgt, order, dq, dk, dv):
    at_row = lax.broadcasted_iota(jnp.int32, (CHUNK, CHUNK), 0)
    at_col = lax.broadcasted_iota(jnp.int32, (CHUNK, CHUNK), 1)
    upper = at_row <= at_col
    lower = at_row >= at_col
    for n in range(count):
        for h in range(HEADS):
            tok = slice((first + n) * CHUNK, (first + n + 1) * CHUNK)
            out = slice(n * CHUNK, (n + 1) * CHUNK)
            kk, vv, gg = (x[h, tok, :] for x in (ks, vs, gs))
            qq = qs[h, out, :]

            def finish(score, keep, left, right, state):
                near = pair(jnp.where(keep, halves(score), 0.0))
                return halves(mm(near, twice(right)) + mm(left, twice(state)))

            dq[h, out, :] = finish(mm(gg, stacked(vv), ROWS), lower, gg, kk, pt[n, h])
            dk[h, out, :] = finish(mm(vv, stacked(gg), ROWS), upper, vv, qq, sgt[n, h])
            dv[h, out, :] = finish(mm(kk, stacked(qq), ROWS), upper, kk, gg, sg[n, h])


def outside_kernel(ks, vs, gs, entered, got, *rest):
    partial = rest[: 3 * SLICES]
    outs = rest[3 * SLICES : 3 * SLICES + 3]
    obs = rest[3 * SLICES + 3 : -1]
    sems = rest[-1]
    sizes, firsts = cut_sizes(ks.shape[1] // CHUNK)
    even = lax.rem(lax.axis_index("seq"), 2) == 0
    weights = []
    for h in range(HEADS):
        before = jnp.where(even, entered[h], got[h])
        after = jnp.where(even, got[h], entered[h])
        weights.append([twice(pair(w)) for w in (before, after.T, after)])

    def send(j, i):
        rows = pl.ds(firsts[i] * CHUNK * HEADS, sizes[i] * CHUNK * HEADS)
        return pltpu.make_async_copy(obs[i].at[j], outs[j].at[rows], sems.at[j, i])

    for j in range(3):
        for i in range(SLICES):
            tile = sizes[i] * CHUNK
            base = firsts[i] * CHUNK
            for h in range(HEADS):
                x = halves(mm((gs, vs, ks)[j][h, base : base + tile, :], weights[h][j]))
                obs[i][j, pl.ds(h, tile, HEADS), :] = x + partial[3 * i + j][h]
            send(j, i).start()
    for j in range(3):
        for i in range(SLICES):
            send(j, i).wait()


VM = pl.BlockSpec(memory_space=pltpu.VMEM)
ANY = pl.BlockSpec(memory_space=pl.ANY)


def vmem(*arrays):
    return [pltpu.with_memory_space_constraint(a, pltpu.VMEM) for a in arrays]


def hbm(*arrays):
    return [pltpu.with_memory_space_constraint(a, pltpu.HBM) for a in arrays]


def body(sizes, queries, key_vectors, value_vectors, grad_output):
    tokens = queries.shape[0]
    chunks = tokens // CHUNK
    flat = [x.reshape(tokens * HEADS, HEAD) for x in (queries, key_vectors, value_vectors, grad_output)]

    tile = 512
    split_shape = pltpu.VMEM((HEADS, tokens, 2 * HEAD), BF16)
    cuts, firsts = cut_sizes(chunks)
    query_shapes = [pltpu.VMEM((HEADS, n * CHUNK, 2 * HEAD), BF16) for n in cuts]
    state_shapes = [pltpu.VMEM((n, HEADS, HEAD, 2 * HEAD), BF16) for n in cuts]
    own_shape = pltpu.VMEM((HEADS, HEAD, HEAD), F32)
    shapes = [split_shape] * 3 + [own_shape] * 2 + query_shapes + state_shapes * 3
    ks, vs, gs, mine, other, *kept = pl.pallas_call(
        functools.partial(states_kernel, tile),
        out_shape=shapes,
        in_specs=[ANY] * 4,
        out_specs=[VM] * len(shapes),
        scratch_shapes=[pltpu.VMEM((tokens // tile, tile * HEADS, HEAD), F32)] * 4
        + [pltpu.VMEM((2, HEADS, HEAD, HEAD), F32), pltpu.SemaphoreType.DMA((4, tokens // tile))],
        compiler_params=pltpu.CompilerParams(vmem_limit_bytes=20 * MIB),
        cost_estimate=pl.CostEstimate(flops=10**9, bytes_accessed=16 * MIB, transcendentals=0),
        name="states",
    )(*hbm(*flat))

    def small(kernel, name, outs, *args):
        return pl.pallas_call(
            kernel,
            out_shape=[own_shape] * outs,
            in_specs=[VM] * len(args),
            out_specs=[VM] * outs,
            compiler_params=pltpu.CompilerParams(vmem_limit_bytes=2 * MIB),
            cost_estimate=pl.CostEstimate(flops=10**5, bytes_accessed=MIB, transcendentals=0),
            name=name,
        )(*vmem(*args))

    partial = []

    def inside(order):
        at = len(partial) // 3
        n = cuts[at]
        made = pl.pallas_call(
            functools.partial(inside_kernel, firsts[at], n),
            out_shape=[pltpu.VMEM((HEADS, n * CHUNK, HEAD), F32)] * 3,
            in_specs=[VM] * 8,
            out_specs=[VM] * 3,
            compiler_params=pltpu.CompilerParams(vmem_limit_bytes=4 * MIB),
            cost_estimate=pl.CostEstimate(flops=n * 4 * 10**8, bytes_accessed=MIB, transcendentals=0),
            name="inside" + str(at),
        )(*vmem(kept[at], ks, vs, gs, *kept[SLICES + at :: SLICES], order))
        partial.extend(made)
        return made[0]

    devices = sizes["seq"]
    sibling = [(i, i ^ 1) for i in range(devices)]
    got = lax.ppermute(other, "seq", sibling)
    (total,) = small(first_kernel, "first", 1, mine, got, inside(other))
    entered = []
    step = 2
    while step < devices:
        got = lax.ppermute(total, "seq", [(i, i ^ step) for i in range(devices)])
        kernel = functools.partial(scan_kernel, step, step == 2, step * 2 >= devices)
        total, *entered = small(kernel, "scan" + str(step), 2, mine, total, got, inside(total), *entered)
        step *= 2
    got = lax.ppermute(total, "seq", sibling)
    while len(partial) < 3 * SLICES:
        inside(total)

    out = pl.pallas_call(
        outside_kernel,
        out_shape=[pltpu.HBM((tokens * HEADS, HEAD), F32)] * 3,
        in_specs=[VM] * (5 + 3 * SLICES),
        out_specs=[ANY] * 3,
        scratch_shapes=[pltpu.VMEM((3, n * CHUNK * HEADS, HEAD), F32) for n in cuts]
        + [pltpu.SemaphoreType.DMA((3, SLICES))],
        compiler_params=pltpu.CompilerParams(vmem_limit_bytes=14 * MIB),
        cost_estimate=pl.CostEstimate(flops=10**9, bytes_accessed=12 * MIB, transcendentals=0),
        name="outside",
    )(*vmem(ks, vs, gs, *entered, got, *partial))
    return tuple(x.reshape(queries.shape) for x in out)


def solution(mesh):
    spec = P(("seqs", "seq"), None, None)
    return jax.shard_map(
        functools.partial(body, dict(mesh.shape)),
        mesh=mesh,
        in_specs=(spec,) * 4,
        out_specs=(spec,) * 3,
        check_vma=False,
    )
```

```python
import functools
import math

import jax
import jax.numpy as jnp
from jax import lax
from jax.experimental import pallas as pl
from jax.experimental.pallas import tpu as pltpu
from jax.sharding import PartitionSpec as P

HEAD = 128
HEADS = 2
CHUNK = 128
CUTS = (3, 13, 13, 3)
SLICES = len(CUTS)

BF16 = jnp.bfloat16
F32 = jnp.float32
NAT = (((1,), (0,)), ((), ()))
ROWS = (((1,), (1,)), ((), ()))
COLS = (((0,), (0,)), ((), ()))
MIB = 1024 * 1024


def cut_sizes(chunks):
    edges = [sum(CUTS[:i]) * chunks // sum(CUTS) for i in range(SLICES + 1)]
    return [b - a for a, b in zip(edges, edges[1:])], edges[:-1]


def mm(a, b, dims=NAT):
    return lax.dot_general(a, b, dims, preferred_element_type=F32)


def parts(x):
    hi = x.astype(BF16)
    lo = (x - hi.astype(F32)).astype(BF16)
    return hi, lo


def pair(x):
    return jnp.concatenate(parts(x), axis=1)


def stacked(xx):
    hi, lo = xx[:, :HEAD], xx[:, HEAD:]
    top = jnp.concatenate([hi, hi], axis=1)
    low = jnp.concatenate([lo, lo], axis=1)
    return jnp.concatenate([top, low], axis=0)


def halves(x):
    return x[:, :HEAD] + x[:, HEAD:]


def twice(xx):
    return jnp.concatenate([xx, xx], axis=0)


def gram(hi, lo, yy):
    return halves(mm(jnp.concatenate([hi, lo], axis=0), twice(yy), COLS))


def states_kernel(tile, q, k, v, g, ks, vs, gs, mine, other, *rest):
    qs, pt, sg, sgt = (rest[j * SLICES : (j + 1) * SLICES] for j in range(4))
    kb, vb, qb, gb, own, sems = rest[4 * SLICES :]
    tokens = q.shape[0] // HEADS
    steps = tokens // tile
    rows = tile * HEADS
    per = tile // CHUNK
    place = [(i, n) for i, size in enumerate(cut_sizes(tokens // CHUNK)[0]) for n in range(size)]

    def fetch(step):
        back = steps - 1 - step
        return [
            pltpu.make_async_copy(src.at[pl.ds(at * rows, rows)], dst.at[step], sems.at[j, step])
            for j, (src, dst, at) in enumerate(((k, kb, step), (v, vb, step), (q, qb, back), (g, gb, back)))
        ]

    for step in range(steps):
        for c in fetch(step):
            c.start()
    core = lax.rem(lax.axis_index("seq"), 2)
    own[...] = jnp.zeros_like(own)
    for step in range(steps):
        for c in fetch(step):
            c.wait()
        back = steps - 1 - step
        for h in range(HEADS):
            p, s = own[0, h], own[1, h]
            for c in range(per):
                n = step * per + c
                tok = slice(n * CHUNK, (n + 1) * CHUNK)
                inside = pl.ds(c * CHUNK * HEADS + h, CHUNK, HEADS)
                kk = pair(kb[step, inside, :])
                vhi, vlo = parts(vb[step, inside, :])
                ks[h, tok, :] = kk
                vs[h, tok, :] = jnp.concatenate([vhi, vlo], axis=1)
                i, m = place[n]
                pt[i][m, h] = pair(p)
                p = p + gram(vhi, vlo, kk)

                r = per - 1 - c
                n = back * per + r
                tok = slice(n * CHUNK, (n + 1) * CHUNK)
                inside = pl.ds(r * CHUNK * HEADS + h, CHUNK, HEADS)
                qhi, qlo = parts(qb[step, inside, :])
                gg = pair(gb[step, inside, :])
                i, m = place[n]
                qs[i][h, m * CHUNK : (m + 1) * CHUNK, :] = jnp.concatenate([qhi, qlo], axis=1)
                gs[h, tok, :] = gg
                shi, slo = parts(s)
                sg[i][m, h] = jnp.concatenate([shi, slo], axis=1)
                sgt[i][m, h] = jnp.concatenate([shi.T, slo.T], axis=1)
                s = s + gram(qhi, qlo, gg)
            own[0, h] = p
            own[1, h] = s
    mine[...] = own[core]
    other[...] = own[1 - core]


def partners(here, low, high, second):
    core = here % 2
    step = low + (high - low) * (core + second - 2 * core * second)
    return [here ^ (k * step) for k in range(1, 4)]


def first_kernel(mine, got, order, chip):
    chip[...] = mine[...] + got[...]


def middle_kernel(low, high, chip, *rest):
    *got, order, entered, m0, m1, m2 = rest
    here = lax.axis_index("seq")

    def rows(low_first):
        first = [here ^ (k * (low if low_first else high)) for k in range(1, 4)]
        second = [here ^ (k * (high if low_first else low)) for k in range(1, 4)]
        return first, second

    @pl.when(lax.rem(here, 2) == 0)
    def _():
        first, _ = rows(True)
        new = sum(g[...] * jnp.where(p < here, 1.0, 0.0) for g, p in zip(got, first))
        entered[...] = new
        total = chip[...] + got[0][...] + got[1][...] + got[2][...]
        for m in (m0, m1, m2):
            m[...] = total

    @pl.when(lax.rem(here, 2) == 1)
    def _():
        first, second = rows(False)
        new = sum(g[...] * jnp.where(p > here, 1.0, 0.0) for g, p in zip(got, first))
        entered[...] = new
        for m, p in zip((m0, m1, m2), second):
            m[...] = new + chip[...] * jnp.where(p < here, 1.0, 0.0)


def last_kernel(high, mine, before, *rest):
    *got, order, entered, message = rest
    here = lax.axis_index("seq")
    new = before[...]
    for k, g in enumerate(got):
        use = (lax.rem(here, 2) == 1) | ((here ^ ((k + 1) * high)) < here)
        new += g[...] * jnp.where(use, 1.0, 0.0)
    entered[...] = new
    message[...] = new + mine[...]


def inside_kernel(first, count, qs, ks, vs, gs, pt, sg, sgt, order, dq, dk, dv):
    at_row = lax.broadcasted_iota(jnp.int32, (CHUNK, CHUNK), 0)
    at_col = lax.broadcasted_iota(jnp.int32, (CHUNK, CHUNK), 1)
    upper = at_row <= at_col
    lower = at_row >= at_col
    for n in range(count):
        for h in range(HEADS):
            tok = slice((first + n) * CHUNK, (first + n + 1) * CHUNK)
            out = slice(n * CHUNK, (n + 1) * CHUNK)
            kk, vv, gg = (x[h, tok, :] for x in (ks, vs, gs))
            qq = qs[h, out, :]

            def finish(score, keep, left, right, state):
                near = pair(jnp.where(keep, halves(score), 0.0))
                return halves(mm(near, twice(right)) + mm(left, twice(state)))

            dq[h, out, :] = finish(mm(gg, stacked(vv), ROWS), lower, gg, kk, pt[n, h])
            dk[h, out, :] = finish(mm(vv, stacked(gg), ROWS), upper, vv, qq, sgt[n, h])
            dv[h, out, :] = finish(mm(kk, stacked(qq), ROWS), upper, kk, gg, sg[n, h])


def outside_kernel(ks, vs, gs, entered, got, *rest):
    partial = rest[: 3 * SLICES]
    outs = rest[3 * SLICES : 3 * SLICES + 3]
    obs = rest[3 * SLICES + 3 : -1]
    sems = rest[-1]
    sizes, firsts = cut_sizes(ks.shape[1] // CHUNK)
    even = lax.rem(lax.axis_index("seq"), 2) == 0
    weights = []
    for h in range(HEADS):
        before = jnp.where(even, entered[h], got[h])
        after = jnp.where(even, got[h], entered[h])
        weights.append([twice(pair(w)) for w in (before, after.T, after)])

    def send(j, i):
        rows = pl.ds(firsts[i] * CHUNK * HEADS, sizes[i] * CHUNK * HEADS)
        return pltpu.make_async_copy(obs[i].at[j], outs[j].at[rows], sems.at[j, i])

    for j in range(3):
        for i in range(SLICES):
            tile = sizes[i] * CHUNK
            base = firsts[i] * CHUNK
            for h in range(HEADS):
                x = halves(mm((gs, vs, ks)[j][h, base : base + tile, :], weights[h][j]))
                obs[i][j, pl.ds(h, tile, HEADS), :] = x + partial[3 * i + j][h]
            send(j, i).start()
    for j in range(3):
        for i in range(SLICES):
            send(j, i).wait()


VM = pl.BlockSpec(memory_space=pltpu.VMEM)
ANY = pl.BlockSpec(memory_space=pl.ANY)


def vmem(*arrays):
    return [pltpu.with_memory_space_constraint(a, pltpu.VMEM) for a in arrays]


def hbm(*arrays):
    return [pltpu.with_memory_space_constraint(a, pltpu.HBM) for a in arrays]


def body(sizes, queries, key_vectors, value_vectors, grad_output):
    tokens = queries.shape[0]
    chunks = tokens // CHUNK
    flat = [x.reshape(tokens * HEADS, HEAD) for x in (queries, key_vectors, value_vectors, grad_output)]

    tile = 512
    split_shape = pltpu.VMEM((HEADS, tokens, 2 * HEAD), BF16)
    cuts, firsts = cut_sizes(chunks)
    query_shapes = [pltpu.VMEM((HEADS, n * CHUNK, 2 * HEAD), BF16) for n in cuts]
    state_shapes = [pltpu.VMEM((n, HEADS, HEAD, 2 * HEAD), BF16) for n in cuts]
    own_shape = pltpu.VMEM((HEADS, HEAD, HEAD), F32)
    shapes = [split_shape] * 3 + [own_shape] * 2 + query_shapes + state_shapes * 3
    ks, vs, gs, mine, other, *kept = pl.pallas_call(
        functools.partial(states_kernel, tile),
        out_shape=shapes,
        in_specs=[ANY] * 4,
        out_specs=[VM] * len(shapes),
        scratch_shapes=[pltpu.VMEM((tokens // tile, tile * HEADS, HEAD), F32)] * 4
        + [pltpu.VMEM((2, HEADS, HEAD, HEAD), F32), pltpu.SemaphoreType.DMA((4, tokens // tile))],
        compiler_params=pltpu.CompilerParams(vmem_limit_bytes=20 * MIB),
        cost_estimate=pl.CostEstimate(flops=10**9, bytes_accessed=16 * MIB, transcendentals=0),
        name="states",
    )(*hbm(*flat))

    def small(kernel, name, outs, *args):
        return pl.pallas_call(
            kernel,
            out_shape=[own_shape] * outs,
            in_specs=[VM] * len(args),
            out_specs=[VM] * outs,
            compiler_params=pltpu.CompilerParams(vmem_limit_bytes=2 * MIB),
            cost_estimate=pl.CostEstimate(flops=10**5, bytes_accessed=MIB, transcendentals=0),
            name=name,
        )(*vmem(*args))

    partial = []

    def inside(order):
        at = len(partial) // 3
        n = cuts[at]
        made = pl.pallas_call(
            functools.partial(inside_kernel, firsts[at], n),
            out_shape=[pltpu.VMEM((HEADS, n * CHUNK, HEAD), F32)] * 3,
            in_specs=[VM] * 8,
            out_specs=[VM] * 3,
            compiler_params=pltpu.CompilerParams(vmem_limit_bytes=4 * MIB),
            cost_estimate=pl.CostEstimate(flops=n * 4 * 10**8, bytes_accessed=MIB, transcendentals=0),
            name="inside" + str(at),
        )(*vmem(kept[at], ks, vs, gs, *kept[SLICES + at :: SLICES], order))
        partial.extend(made)
        return made[0]

    devices = sizes["seq"]
    sibling = [(i, i ^ 1) for i in range(devices)]
    got = lax.ppermute(other, "seq", sibling)
    (chip,) = small(first_kernel, "first", 1, mine, got, inside(other))

    side = math.isqrt(devices // 2)
    low, high = 2, 2 * side

    def swap(messages, second):
        out = []
        for k, m in enumerate(messages):
            pairs = [(d, partners(d, low, high, second)[k]) for d in range(devices)]
            out.append(lax.ppermute(m, "seq", pairs))
        return out

    got = swap([chip] * 3, 0)
    entered, *messages = small(functools.partial(middle_kernel, low, high), "middle", 4, chip, *got, inside(chip))
    got = swap(messages, 1)
    kernel = functools.partial(last_kernel, high)
    entered, message = small(kernel, "last", 2, mine, entered, *got, inside(messages[0]))
    got = lax.ppermute(message, "seq", sibling)
    while len(partial) < 3 * SLICES:
        inside(message)

    out = pl.pallas_call(
        outside_kernel,
        out_shape=[pltpu.HBM((tokens * HEADS, HEAD), F32)] * 3,
        in_specs=[VM] * (5 + 3 * SLICES),
        out_specs=[ANY] * 3,
        scratch_shapes=[pltpu.VMEM((3, n * CHUNK * HEADS, HEAD), F32) for n in cuts]
        + [pltpu.SemaphoreType.DMA((3, SLICES))],
        compiler_params=pltpu.CompilerParams(vmem_limit_bytes=14 * MIB),
        cost_estimate=pl.CostEstimate(flops=10**9, bytes_accessed=12 * MIB, transcendentals=0),
        name="outside",
    )(*vmem(ks, vs, gs, entered, got, *partial))
    return tuple(x.reshape(queries.shape) for x in out)


def solution(mesh):
    spec = P(("seqs", "seq"), None, None)
    return jax.shard_map(
        functools.partial(body, dict(mesh.shape)),
        mesh=mesh,
        in_specs=(spec,) * 4,
        out_specs=(spec,) * 3,
        check_vma=False,
    )
```

```python
import functools
import math

import jax
import jax.numpy as jnp
from jax import lax
from jax.experimental import pallas as pl
from jax.experimental.pallas import tpu as pltpu
from jax.sharding import PartitionSpec as P

HEAD = 128
HEADS = 2
CHUNK = 128
CUTS = (3, 13, 13, 3)
LEAD = 4
PIECE = 5
SLICES = len(CUTS)

BF16 = jnp.bfloat16
F32 = jnp.float32
NAT = (((1,), (0,)), ((), ()))
ROWS = (((1,), (1,)), ((), ()))
COLS = (((0,), (0,)), ((), ()))
MIB = 1024 * 1024


def cut_sizes(chunks):
    edges = [sum(CUTS[:i]) * chunks // sum(CUTS) for i in range(SLICES + 1)]
    return [b - a for a, b in zip(edges, edges[1:])], edges[:-1]


def piece_list(sizes):
    pieces = []
    for i, size in enumerate(sizes):
        count = -(-size // PIECE)
        edges = [size * n // count for n in range(count + 1)]
        pieces += [(i, a, b - a) for a, b in zip(edges, edges[1:])]
    return pieces


def mm(a, b, dims=NAT):
    return lax.dot_general(a, b, dims, preferred_element_type=F32)


def parts(x):
    hi = x.astype(BF16)
    lo = (x - hi.astype(F32)).astype(BF16)
    return hi, lo


def pair(x):
    return jnp.concatenate(parts(x), axis=1)


def stacked(xx):
    hi, lo = xx[:, :HEAD], xx[:, HEAD:]
    top = jnp.concatenate([hi, hi], axis=1)
    low = jnp.concatenate([lo, lo], axis=1)
    return jnp.concatenate([top, low], axis=0)


def halves(x):
    return x[:, :HEAD] + x[:, HEAD:]


def twice(xx):
    return jnp.concatenate([xx, xx], axis=0)


def gram(hi, lo, yy):
    return halves(mm(jnp.concatenate([hi, lo], axis=0), twice(yy), COLS))


def states_kernel(tile, q, k, v, g, ks, vs, gs, mine, other, *rest):
    qs, pt, sg, sgt = (rest[j * SLICES : (j + 1) * SLICES] for j in range(4))
    kb, vb, qb, gb, own, sems = rest[4 * SLICES :]
    tokens = q.shape[0] // HEADS
    steps = tokens // tile
    rows = tile * HEADS
    per = tile // CHUNK
    place = [(i, n) for i, size in enumerate(cut_sizes(tokens // CHUNK)[0]) for n in range(size)]

    def fetch(step):
        back = steps - 1 - step
        return [
            pltpu.make_async_copy(src.at[pl.ds(at * rows, rows)], dst.at[step], sems.at[j, step])
            for j, (src, dst, at) in enumerate(((k, kb, step), (v, vb, step), (q, qb, back), (g, gb, back)))
        ]

    for step in range(steps):
        for c in fetch(step):
            c.start()
    core = lax.rem(lax.axis_index("seq"), 2)
    own[...] = jnp.zeros_like(own)
    for step in range(steps):
        for c in fetch(step):
            c.wait()
        back = steps - 1 - step
        for h in range(HEADS):
            p, s = own[0, h], own[1, h]
            for c in range(per):
                n = step * per + c
                tok = slice(n * CHUNK, (n + 1) * CHUNK)
                inside = pl.ds(c * CHUNK * HEADS + h, CHUNK, HEADS)
                kk = pair(kb[step, inside, :])
                vhi, vlo = parts(vb[step, inside, :])
                ks[h, tok, :] = kk
                vs[h, tok, :] = jnp.concatenate([vhi, vlo], axis=1)
                i, m = place[n]
                pt[i][m, h] = pair(p)
                p = p + gram(vhi, vlo, kk)

                r = per - 1 - c
                n = back * per + r
                tok = slice(n * CHUNK, (n + 1) * CHUNK)
                inside = pl.ds(r * CHUNK * HEADS + h, CHUNK, HEADS)
                qhi, qlo = parts(qb[step, inside, :])
                gg = pair(gb[step, inside, :])
                i, m = place[n]
                qs[i][h, m * CHUNK : (m + 1) * CHUNK, :] = jnp.concatenate([qhi, qlo], axis=1)
                gs[h, tok, :] = gg
                shi, slo = parts(s)
                sg[i][m, h] = jnp.concatenate([shi, slo], axis=1)
                sgt[i][m, h] = jnp.concatenate([shi.T, slo.T], axis=1)
                s = s + gram(qhi, qlo, gg)
            own[0, h] = p
            own[1, h] = s
    mine[...] = own[core]
    other[...] = own[1 - core]


def partners(here, low, high, second):
    core = here % 2
    step = low + (high - low) * (core + second - 2 * core * second)
    return [here ^ (k * step) for k in range(1, 4)]


def first_kernel(mine, got, order, *chip):
    new = mine[...] + got[...]
    for c in chip:
        c[...] = new


def middle_kernel(low, high, chip, *rest):
    *got, order, entered, m0, m1, m2 = rest
    here = lax.axis_index("seq")

    def rows(low_first):
        first = [here ^ (k * (low if low_first else high)) for k in range(1, 4)]
        second = [here ^ (k * (high if low_first else low)) for k in range(1, 4)]
        return first, second

    @pl.when(lax.rem(here, 2) == 0)
    def _():
        first, _ = rows(True)
        new = sum(g[...] * jnp.where(p < here, 1.0, 0.0) for g, p in zip(got, first))
        entered[...] = new
        total = chip[...] + got[0][...] + got[1][...] + got[2][...]
        for m in (m0, m1, m2):
            m[...] = total

    @pl.when(lax.rem(here, 2) == 1)
    def _():
        first, second = rows(False)
        new = sum(g[...] * jnp.where(p > here, 1.0, 0.0) for g, p in zip(got, first))
        entered[...] = new
        for m, p in zip((m0, m1, m2), second):
            m[...] = new + chip[...] * jnp.where(p < here, 1.0, 0.0)


def last_kernel(high, mine, before, *rest):
    *got, order, entered, message = rest
    here = lax.axis_index("seq")
    new = before[...]
    for k, g in enumerate(got):
        use = (lax.rem(here, 2) == 1) | ((here ^ ((k + 1) * high)) < here)
        new += g[...] * jnp.where(use, 1.0, 0.0)
    entered[...] = new
    message[...] = new + mine[...]


def inside_kernel(first, count, qs, ks, vs, gs, pt, sg, sgt, order, dq, dk, dv):
    at_row = lax.broadcasted_iota(jnp.int32, (CHUNK, CHUNK), 0)
    at_col = lax.broadcasted_iota(jnp.int32, (CHUNK, CHUNK), 1)
    upper = at_row <= at_col
    lower = at_row >= at_col
    work = [(n, h, which) for n in range(count) for h in range(HEADS) for which in range(3)]

    def load(n, h):
        tok = slice((first + n) * CHUNK, (first + n + 1) * CHUNK)
        return qs[h, n * CHUNK : (n + 1) * CHUNK, :], ks[h, tok, :], vs[h, tok, :], gs[h, tok, :]

    def score(n, h, which):
        qq, kk, vv, gg = load(n, h)
        a, b = ((gg, vv), (vv, gg), (kk, qq))[which]
        return halves(mm(a, stacked(b), ROWS))

    def finish(near, n, h, which):
        qq, kk, vv, gg = load(n, h)
        keep, left, right, state, out = (
            (lower, gg, kk, pt, dq),
            (upper, vv, qq, sgt, dk),
            (upper, kk, gg, sg, dv),
        )[which]
        hi, lo = parts(jnp.where(keep, near, 0.0))
        top = jnp.concatenate([hi, left[:, :HEAD]], axis=1)
        low = jnp.concatenate([lo, left[:, HEAD:]], axis=1)
        x = mm(jnp.concatenate([top, low], axis=0), jnp.concatenate([right, state[n, h]], axis=0))
        out[h, n * CHUNK : (n + 1) * CHUNK, :] = halves(x[:CHUNK]) + x[CHUNK:, :HEAD]

    ready = []
    for i in range(len(work) + LEAD):
        if i < len(work):
            ready.append(score(*work[i]))
        if i >= LEAD:
            finish(ready.pop(0), *work[i - LEAD])


def outside_kernel(ks, vs, gs, entered, got, *rest):
    partial = rest[: 3 * SLICES]
    outs = rest[3 * SLICES : 3 * SLICES + 3]
    obs = rest[3 * SLICES + 3 : -1]
    sems = rest[-1]
    sizes, firsts = cut_sizes(ks.shape[1] // CHUNK)
    pieces = piece_list(sizes)
    even = lax.rem(lax.axis_index("seq"), 2) == 0
    weights = []
    for h in range(HEADS):
        before = jnp.where(even, entered[h], got[h])
        after = jnp.where(even, got[h], entered[h])
        weights.append([twice(pair(w)) for w in (before, after.T, after)])

    def send(j, n):
        i, first, size = pieces[n]
        src = obs[i].at[j, pl.ds(first * CHUNK * HEADS, size * CHUNK * HEADS)]
        dst = outs[j].at[pl.ds((firsts[i] + first) * CHUNK * HEADS, size * CHUNK * HEADS)]
        return pltpu.make_async_copy(src, dst, sems.at[j, n])

    work = [(j, n) for j in range(3) for n in range(len(pieces))]
    for j, n in work:
        i, first, size = pieces[n]
        tile = size * CHUNK
        off = first * CHUNK
        base = firsts[i] * CHUNK + off
        for h in range(HEADS):
            x = halves(mm((gs, vs, ks)[j][h, base : base + tile, :], weights[h][j]))
            obs[i][j, pl.ds(off * HEADS + h, tile, HEADS), :] = x + partial[3 * i + j][h, off : off + tile, :]
        send(j, n).start()
    for j, n in work:
        send(j, n).wait()


VM = pl.BlockSpec(memory_space=pltpu.VMEM)
ANY = pl.BlockSpec(memory_space=pl.ANY)


def vmem(*arrays):
    return [pltpu.with_memory_space_constraint(a, pltpu.VMEM) for a in arrays]


def hbm(*arrays):
    return [pltpu.with_memory_space_constraint(a, pltpu.HBM) for a in arrays]


def body(sizes, queries, key_vectors, value_vectors, grad_output):
    tokens = queries.shape[0]
    chunks = tokens // CHUNK
    flat = [x.reshape(tokens * HEADS, HEAD) for x in (queries, key_vectors, value_vectors, grad_output)]

    tile = 512
    split_shape = pltpu.VMEM((HEADS, tokens, 2 * HEAD), BF16)
    cuts, firsts = cut_sizes(chunks)
    query_shapes = [pltpu.VMEM((HEADS, n * CHUNK, 2 * HEAD), BF16) for n in cuts]
    state_shapes = [pltpu.VMEM((n, HEADS, HEAD, 2 * HEAD), BF16) for n in cuts]
    own_shape = pltpu.VMEM((HEADS, HEAD, HEAD), F32)
    shapes = [split_shape] * 3 + [own_shape] * 2 + query_shapes + state_shapes * 3
    ks, vs, gs, mine, other, *kept = pl.pallas_call(
        functools.partial(states_kernel, tile),
        out_shape=shapes,
        in_specs=[ANY] * 4,
        out_specs=[VM] * len(shapes),
        scratch_shapes=[pltpu.VMEM((tokens // tile, tile * HEADS, HEAD), F32)] * 4
        + [pltpu.VMEM((2, HEADS, HEAD, HEAD), F32), pltpu.SemaphoreType.DMA((4, tokens // tile))],
        compiler_params=pltpu.CompilerParams(vmem_limit_bytes=20 * MIB),
        cost_estimate=pl.CostEstimate(flops=10**9, bytes_accessed=16 * MIB, transcendentals=0),
        name="states",
    )(*hbm(*flat))

    def small(kernel, name, outs, *args):
        return pl.pallas_call(
            kernel,
            out_shape=[own_shape] * outs,
            in_specs=[VM] * len(args),
            out_specs=[VM] * outs,
            compiler_params=pltpu.CompilerParams(vmem_limit_bytes=2 * MIB),
            cost_estimate=pl.CostEstimate(flops=10**5, bytes_accessed=MIB, transcendentals=0),
            name=name,
        )(*vmem(*args))

    partial = []

    def inside(order):
        at = len(partial) // 3
        n = cuts[at]
        made = pl.pallas_call(
            functools.partial(inside_kernel, firsts[at], n),
            out_shape=[pltpu.VMEM((HEADS, n * CHUNK, HEAD), F32)] * 3,
            in_specs=[VM] * 8,
            out_specs=[VM] * 3,
            compiler_params=pltpu.CompilerParams(vmem_limit_bytes=4 * MIB),
            cost_estimate=pl.CostEstimate(flops=n * 4 * 10**8, bytes_accessed=MIB, transcendentals=0),
            name="inside" + str(at),
        )(*vmem(kept[at], ks, vs, gs, *kept[SLICES + at :: SLICES], order))
        partial.extend(made)
        return made[0]

    devices = sizes["seq"]
    sibling = [(i, i ^ 1) for i in range(devices)]
    got = lax.ppermute(other, "seq", sibling)
    chips = small(first_kernel, "first", 3, mine, got, inside(other))

    side = math.isqrt(devices // 2)
    low, high = 2, 2 * side

    def swap(messages, second):
        out = []
        for k, m in enumerate(messages):
            pairs = [(d, partners(d, low, high, second)[k]) for d in range(devices)]
            out.append(lax.ppermute(m, "seq", pairs))
        return out

    got = swap(chips, 0)
    entered, *messages = small(functools.partial(middle_kernel, low, high), "middle", 4, chips[0], *got, inside(chips[0]))
    got = swap(messages, 1)
    kernel = functools.partial(last_kernel, high)
    entered, message = small(kernel, "last", 2, mine, entered, *got, inside(messages[0]))
    got = lax.ppermute(message, "seq", sibling)
    while len(partial) < 3 * SLICES:
        inside(message)

    out = pl.pallas_call(
        outside_kernel,
        out_shape=[pltpu.HBM((tokens * HEADS, HEAD), F32)] * 3,
        in_specs=[VM] * (5 + 3 * SLICES),
        out_specs=[ANY] * 3,
        scratch_shapes=[pltpu.VMEM((3, n * CHUNK * HEADS, HEAD), F32) for n in cuts]
        + [pltpu.SemaphoreType.DMA((3, len(piece_list(cuts))))],
        compiler_params=pltpu.CompilerParams(vmem_limit_bytes=14 * MIB),
        cost_estimate=pl.CostEstimate(flops=10**9, bytes_accessed=12 * MIB, transcendentals=0),
        name="outside",
    )(*vmem(ks, vs, gs, entered, got, *partial))
    return tuple(x.reshape(queries.shape) for x in out)


def solution(mesh):
    spec = P(("seqs", "seq"), None, None)
    return jax.shard_map(
        functools.partial(body, dict(mesh.shape)),
        mesh=mesh,
        in_specs=(spec,) * 4,
        out_specs=(spec,) * 3,
        check_vma=False,
    )
```

```python
import functools
import math

import jax
import jax.numpy as jnp
from jax import lax
from jax.experimental import pallas as pl
from jax.experimental.pallas import tpu as pltpu
from jax.sharding import PartitionSpec as P

HEAD = 128
HEADS = 2
CHUNK = 128
CUTS = (2, 14, 14, 2)
LEAD = 4
PIECE = 5
SLICES = len(CUTS)

BF16 = jnp.bfloat16
F32 = jnp.float32
NAT = (((1,), (0,)), ((), ()))
ROWS = (((1,), (1,)), ((), ()))
COLS = (((0,), (0,)), ((), ()))
MIB = 1024 * 1024


def cut_sizes(chunks):
    edges = [sum(CUTS[:i]) * chunks // sum(CUTS) for i in range(SLICES + 1)]
    return [b - a for a, b in zip(edges, edges[1:])], edges[:-1]


def piece_list(sizes):
    pieces = []
    for i, size in enumerate(sizes):
        count = -(-size // PIECE)
        edges = [size * n // count for n in range(count + 1)]
        pieces += [(i, a, b - a) for a, b in zip(edges, edges[1:])]
    return pieces


def mm(a, b, dims=NAT):
    return lax.dot_general(a, b, dims, preferred_element_type=F32)


def parts(x):
    hi = x.astype(BF16)
    lo = (x - hi.astype(F32)).astype(BF16)
    return hi, lo


def pair(x):
    return jnp.concatenate(parts(x), axis=1)


def stacked(xx):
    hi, lo = xx[:, :HEAD], xx[:, HEAD:]
    top = jnp.concatenate([hi, hi], axis=1)
    low = jnp.concatenate([lo, lo], axis=1)
    return jnp.concatenate([top, low], axis=0)


def halves(x):
    return x[:, :HEAD] + x[:, HEAD:]


def twice(xx):
    return jnp.concatenate([xx, xx], axis=0)


def gram(hi, lo, yy):
    return halves(mm(jnp.concatenate([hi, lo], axis=0), twice(yy), COLS))


def states_kernel(tile, q, k, v, g, ks, vs, gs, mine, other, *rest):
    qs, pt, sg, sgt = (rest[j * SLICES : (j + 1) * SLICES] for j in range(4))
    kb, vb, qb, gb, own, sems = rest[4 * SLICES :]
    tokens = q.shape[0] // HEADS
    steps = tokens // tile
    rows = tile * HEADS
    per = tile // CHUNK
    place = [(i, n) for i, size in enumerate(cut_sizes(tokens // CHUNK)[0]) for n in range(size)]

    def fetch(step):
        back = steps - 1 - step
        return [
            pltpu.make_async_copy(src.at[pl.ds(at * rows, rows)], dst.at[step], sems.at[j, step])
            for j, (src, dst, at) in enumerate(((k, kb, step), (v, vb, step), (q, qb, back), (g, gb, back)))
        ]

    for step in range(steps):
        for c in fetch(step):
            c.start()
    core = lax.rem(lax.axis_index("seq"), 2)
    own[...] = jnp.zeros_like(own)
    for step in range(steps):
        for c in fetch(step):
            c.wait()
        back = steps - 1 - step
        for h in range(HEADS):
            p, s = own[0, h], own[1, h]
            for c in range(per):
                n = step * per + c
                tok = slice(n * CHUNK, (n + 1) * CHUNK)
                inside = pl.ds(c * CHUNK * HEADS + h, CHUNK, HEADS)
                kk = pair(kb[step, inside, :])
                vhi, vlo = parts(vb[step, inside, :])
                ks[h, tok, :] = kk
                vs[h, tok, :] = jnp.concatenate([vhi, vlo], axis=1)
                i, m = place[n]
                pt[i][m, h] = pair(p)
                p = p + gram(vhi, vlo, kk)

                r = per - 1 - c
                n = back * per + r
                tok = slice(n * CHUNK, (n + 1) * CHUNK)
                inside = pl.ds(r * CHUNK * HEADS + h, CHUNK, HEADS)
                qhi, qlo = parts(qb[step, inside, :])
                gg = pair(gb[step, inside, :])
                i, m = place[n]
                qs[i][h, m * CHUNK : (m + 1) * CHUNK, :] = jnp.concatenate([qhi, qlo], axis=1)
                gs[h, tok, :] = gg
                shi, slo = parts(s)
                sg[i][m, h] = jnp.concatenate([shi, slo], axis=1)
                sgt[i][m, h] = jnp.concatenate([shi.T, slo.T], axis=1)
                s = s + gram(qhi, qlo, gg)
            own[0, h] = p
            own[1, h] = s
    mine[...] = own[core]
    other[...] = own[1 - core]


def partners(here, low, high, second):
    core = here % 2
    step = low + (high - low) * (core + second - 2 * core * second)
    return [here ^ (k * step) for k in range(1, 4)]


def first_kernel(mine, got, order, *chip):
    new = mine[...] + got[...]
    for c in chip:
        c[...] = new


def middle_kernel(low, high, chip, *rest):
    *got, order, entered, m0, m1, m2 = rest
    here = lax.axis_index("seq")

    def rows(low_first):
        first = [here ^ (k * (low if low_first else high)) for k in range(1, 4)]
        second = [here ^ (k * (high if low_first else low)) for k in range(1, 4)]
        return first, second

    @pl.when(lax.rem(here, 2) == 0)
    def _():
        first, _ = rows(True)
        new = sum(g[...] * jnp.where(p < here, 1.0, 0.0) for g, p in zip(got, first))
        entered[...] = new
        total = chip[...] + got[0][...] + got[1][...] + got[2][...]
        for m in (m0, m1, m2):
            m[...] = total

    @pl.when(lax.rem(here, 2) == 1)
    def _():
        first, second = rows(False)
        new = sum(g[...] * jnp.where(p > here, 1.0, 0.0) for g, p in zip(got, first))
        entered[...] = new
        for m, p in zip((m0, m1, m2), second):
            m[...] = new + chip[...] * jnp.where(p < here, 1.0, 0.0)


def last_kernel(high, mine, before, *rest):
    *got, order, entered, message = rest
    here = lax.axis_index("seq")
    new = before[...]
    for k, g in enumerate(got):
        use = (lax.rem(here, 2) == 1) | ((here ^ ((k + 1) * high)) < here)
        new += g[...] * jnp.where(use, 1.0, 0.0)
    entered[...] = new
    message[...] = new + mine[...]


def inside_kernel(first, count, qs, ks, vs, gs, pt, sg, sgt, order, dq, dk, dv):
    at_row = lax.broadcasted_iota(jnp.int32, (CHUNK, CHUNK), 0)
    at_col = lax.broadcasted_iota(jnp.int32, (CHUNK, CHUNK), 1)
    upper = at_row <= at_col
    lower = at_row >= at_col
    work = [(n, h, which) for n in range(count) for h in range(HEADS) for which in range(3)]

    def load(n, h):
        tok = slice((first + n) * CHUNK, (first + n + 1) * CHUNK)
        return qs[h, n * CHUNK : (n + 1) * CHUNK, :], ks[h, tok, :], vs[h, tok, :], gs[h, tok, :]

    def score(n, h, which):
        qq, kk, vv, gg = load(n, h)
        a, b = ((gg, vv), (vv, gg), (kk, qq))[which]
        return halves(mm(a, stacked(b), ROWS))

    def finish(near, n, h, which):
        qq, kk, vv, gg = load(n, h)
        keep, left, right, state, out = (
            (lower, gg, kk, pt, dq),
            (upper, vv, qq, sgt, dk),
            (upper, kk, gg, sg, dv),
        )[which]
        hi, lo = parts(jnp.where(keep, near, 0.0))
        top = jnp.concatenate([hi, left[:, :HEAD]], axis=1)
        low = jnp.concatenate([lo, left[:, HEAD:]], axis=1)
        x = mm(jnp.concatenate([top, low], axis=0), jnp.concatenate([right, state[n, h]], axis=0))
        out[h, n * CHUNK : (n + 1) * CHUNK, :] = halves(x[:CHUNK]) + x[CHUNK:, :HEAD]

    ready = []
    for i in range(len(work) + LEAD):
        if i < len(work):
            ready.append(score(*work[i]))
        if i >= LEAD:
            finish(ready.pop(0), *work[i - LEAD])


def outside_kernel(ks, vs, gs, entered, got, *rest):
    partial = rest[: 3 * SLICES]
    outs = rest[3 * SLICES : 3 * SLICES + 3]
    obs = rest[3 * SLICES + 3 : -1]
    sems = rest[-1]
    sizes, firsts = cut_sizes(ks.shape[1] // CHUNK)
    pieces = piece_list(sizes)
    even = lax.rem(lax.axis_index("seq"), 2) == 0
    weights = []
    for h in range(HEADS):
        before = jnp.where(even, entered[h], got[h])
        after = jnp.where(even, got[h], entered[h])
        weights.append([twice(pair(w)) for w in (before, after.T, after)])

    def send(j, n):
        i, first, size = pieces[n]
        src = obs[i].at[j, pl.ds(first * CHUNK * HEADS, size * CHUNK * HEADS)]
        dst = outs[j].at[pl.ds((firsts[i] + first) * CHUNK * HEADS, size * CHUNK * HEADS)]
        return pltpu.make_async_copy(src, dst, sems.at[j, n])

    work = [(j, n) for j in range(3) for n in range(len(pieces))]
    for j, n in work:
        i, first, size = pieces[n]
        tile = size * CHUNK
        off = first * CHUNK
        base = firsts[i] * CHUNK + off
        for h in range(HEADS):
            x = halves(mm((gs, vs, ks)[j][h, base : base + tile, :], weights[h][j]))
            obs[i][j, pl.ds(off * HEADS + h, tile, HEADS), :] = x + partial[3 * i + j][h, off : off + tile, :]
        send(j, n).start()
    for j, n in work:
        send(j, n).wait()


VM = pl.BlockSpec(memory_space=pltpu.VMEM)
ANY = pl.BlockSpec(memory_space=pl.ANY)


def vmem(*arrays):
    return [pltpu.with_memory_space_constraint(a, pltpu.VMEM) for a in arrays]


def hbm(*arrays):
    return [pltpu.with_memory_space_constraint(a, pltpu.HBM) for a in arrays]


def body(sizes, queries, key_vectors, value_vectors, grad_output):
    tokens = queries.shape[0]
    chunks = tokens // CHUNK
    flat = [x.reshape(tokens * HEADS, HEAD) for x in (queries, key_vectors, value_vectors, grad_output)]

    tile = 512
    split_shape = pltpu.VMEM((HEADS, tokens, 2 * HEAD), BF16)
    cuts, firsts = cut_sizes(chunks)
    query_shapes = [pltpu.VMEM((HEADS, n * CHUNK, 2 * HEAD), BF16) for n in cuts]
    state_shapes = [pltpu.VMEM((n, HEADS, HEAD, 2 * HEAD), BF16) for n in cuts]
    own_shape = pltpu.VMEM((HEADS, HEAD, HEAD), F32)
    shapes = [split_shape] * 3 + [own_shape] * 2 + query_shapes + state_shapes * 3
    ks, vs, gs, mine, other, *kept = pl.pallas_call(
        functools.partial(states_kernel, tile),
        out_shape=shapes,
        in_specs=[ANY] * 4,
        out_specs=[VM] * len(shapes),
        scratch_shapes=[pltpu.VMEM((tokens // tile, tile * HEADS, HEAD), F32)] * 4
        + [pltpu.VMEM((2, HEADS, HEAD, HEAD), F32), pltpu.SemaphoreType.DMA((4, tokens // tile))],
        compiler_params=pltpu.CompilerParams(vmem_limit_bytes=20 * MIB),
        cost_estimate=pl.CostEstimate(flops=10**9, bytes_accessed=16 * MIB, transcendentals=0),
        name="states",
    )(*hbm(*flat))

    def small(kernel, name, outs, *args):
        return pl.pallas_call(
            kernel,
            out_shape=[own_shape] * outs,
            in_specs=[VM] * len(args),
            out_specs=[VM] * outs,
            compiler_params=pltpu.CompilerParams(vmem_limit_bytes=2 * MIB),
            cost_estimate=pl.CostEstimate(flops=10**5, bytes_accessed=MIB, transcendentals=0),
            name=name,
        )(*vmem(*args))

    partial = []

    def inside(order):
        at = len(partial) // 3
        n = cuts[at]
        made = pl.pallas_call(
            functools.partial(inside_kernel, firsts[at], n),
            out_shape=[pltpu.VMEM((HEADS, n * CHUNK, HEAD), F32)] * 3,
            in_specs=[VM] * 8,
            out_specs=[VM] * 3,
            compiler_params=pltpu.CompilerParams(vmem_limit_bytes=4 * MIB),
            cost_estimate=pl.CostEstimate(flops=n * 4 * 10**8, bytes_accessed=MIB, transcendentals=0),
            name="inside" + str(at),
        )(*vmem(kept[at], ks, vs, gs, *kept[SLICES + at :: SLICES], order))
        partial.extend(made)
        return made[0]

    devices = sizes["seq"]
    sibling = [(i, i ^ 1) for i in range(devices)]
    got = lax.ppermute(other, "seq", sibling)
    chips = small(first_kernel, "first", 3, mine, got, inside(other))

    side = math.isqrt(devices // 2)
    low, high = 2, 2 * side

    def swap(messages, second):
        out = []
        for k, m in enumerate(messages):
            pairs = [(d, partners(d, low, high, second)[k]) for d in range(devices)]
            out.append(lax.ppermute(m, "seq", pairs))
        return out

    got = swap(chips, 0)
    entered, *messages = small(functools.partial(middle_kernel, low, high), "middle", 4, chips[0], *got, inside(chips[0]))
    got = swap(messages, 1)
    kernel = functools.partial(last_kernel, high)
    entered, message = small(kernel, "last", 2, mine, entered, *got, inside(messages[0]))
    got = lax.ppermute(message, "seq", sibling)
    while len(partial) < 3 * SLICES:
        inside(message)

    out = pl.pallas_call(
        outside_kernel,
        out_shape=[pltpu.HBM((tokens * HEADS, HEAD), F32)] * 3,
        in_specs=[VM] * (5 + 3 * SLICES),
        out_specs=[ANY] * 3,
        scratch_shapes=[pltpu.VMEM((3, n * CHUNK * HEADS, HEAD), F32) for n in cuts]
        + [pltpu.SemaphoreType.DMA((3, len(piece_list(cuts))))],
        compiler_params=pltpu.CompilerParams(vmem_limit_bytes=14 * MIB),
        cost_estimate=pl.CostEstimate(flops=10**9, bytes_accessed=12 * MIB, transcendentals=0),
        name="outside",
    )(*vmem(ks, vs, gs, entered, got, *partial))
    return tuple(x.reshape(queries.shape) for x in out)


def solution(mesh):
    spec = P(("seqs", "seq"), None, None)
    return jax.shard_map(
        functools.partial(body, dict(mesh.shape)),
        mesh=mesh,
        in_specs=(spec,) * 4,
        out_specs=(spec,) * 3,
        check_vma=False,
    )
```

```python
import functools
import math

import jax
import jax.numpy as jnp
from jax import lax
from jax.experimental import pallas as pl
from jax.experimental.pallas import tpu as pltpu
from jax.sharding import PartitionSpec as P

HEAD = 128
HEADS = 2
CHUNK = 128
CUTS = (2, 14, 14, 2)
LEAD = 4
PIECE = 5
SLICES = len(CUTS)

BF16 = jnp.bfloat16
F32 = jnp.float32
NAT = (((1,), (0,)), ((), ()))
ROWS = (((1,), (1,)), ((), ()))
COLS = (((0,), (0,)), ((), ()))
MIB = 1024 * 1024


def cut_sizes(chunks):
    edges = [sum(CUTS[:i]) * chunks // sum(CUTS) for i in range(SLICES + 1)]
    return [b - a for a, b in zip(edges, edges[1:])], edges[:-1]


def piece_list(sizes):
    pieces = []
    for i, size in enumerate(sizes):
        count = -(-size // PIECE)
        edges = [size * n // count for n in range(count + 1)]
        pieces += [(i, a, b - a) for a, b in zip(edges, edges[1:])]
    return pieces


def mm(a, b, dims=NAT):
    return lax.dot_general(a, b, dims, preferred_element_type=F32)


def parts(x):
    hi = x.astype(BF16)
    lo = (x - hi.astype(F32)).astype(BF16)
    return hi, lo


def pair(x):
    return jnp.concatenate(parts(x), axis=1)


def stacked(xx):
    hi, lo = xx[:, :HEAD], xx[:, HEAD:]
    top = jnp.concatenate([hi, hi], axis=1)
    low = jnp.concatenate([lo, lo], axis=1)
    return jnp.concatenate([top, low], axis=0)


def halves(x):
    return x[:, :HEAD] + x[:, HEAD:]


def twice(xx):
    return jnp.concatenate([xx, xx], axis=0)


def gram(hi, lo, yy):
    return halves(mm(jnp.concatenate([hi, lo], axis=0), twice(yy), COLS))


def states_kernel(tile, q, k, v, g, ks, vs, gs, mine, other, *rest):
    qs, pt, sg, sgt = (rest[j * SLICES : (j + 1) * SLICES] for j in range(4))
    kb, vb, qb, gb, own, sems = rest[4 * SLICES :]
    tokens = q.shape[0] // HEADS
    steps = tokens // tile
    rows = tile * HEADS
    per = tile // CHUNK
    place = [(i, n) for i, size in enumerate(cut_sizes(tokens // CHUNK)[0]) for n in range(size)]

    def fetch(step):
        back = steps - 1 - step
        return [
            pltpu.make_async_copy(src.at[pl.ds(at * rows, rows)], dst.at[step], sems.at[j, step])
            for j, (src, dst, at) in enumerate(((k, kb, step), (v, vb, step), (q, qb, back), (g, gb, back)))
        ]

    for step in range(steps):
        for c in fetch(step):
            c.start()
    core = lax.rem(lax.axis_index("seq"), 2)
    own[...] = jnp.zeros_like(own)
    for step in range(steps):
        for c in fetch(step):
            c.wait()
        back = steps - 1 - step
        for c in range(per):
            for h in range(HEADS):
                p, s = own[0, h], own[1, h]
                n = step * per + c
                tok = slice(n * CHUNK, (n + 1) * CHUNK)
                inside = pl.ds(c * CHUNK * HEADS + h, CHUNK, HEADS)
                kk = pair(kb[step, inside, :])
                vhi, vlo = parts(vb[step, inside, :])
                ks[h, tok, :] = kk
                vs[h, tok, :] = jnp.concatenate([vhi, vlo], axis=1)
                i, m = place[n]
                pt[i][m, h] = pair(p)
                p = p + gram(vhi, vlo, kk)

                r = per - 1 - c
                n = back * per + r
                tok = slice(n * CHUNK, (n + 1) * CHUNK)
                inside = pl.ds(r * CHUNK * HEADS + h, CHUNK, HEADS)
                qhi, qlo = parts(qb[step, inside, :])
                gg = pair(gb[step, inside, :])
                i, m = place[n]
                qs[i][h, m * CHUNK : (m + 1) * CHUNK, :] = jnp.concatenate([qhi, qlo], axis=1)
                gs[h, tok, :] = gg
                shi, slo = parts(s)
                sg[i][m, h] = jnp.concatenate([shi, slo], axis=1)
                sgt[i][m, h] = jnp.concatenate([shi.T, slo.T], axis=1)
                s = s + gram(qhi, qlo, gg)
                own[0, h] = p
                own[1, h] = s
    mine[...] = own[core]
    other[...] = own[1 - core]


def partners(here, low, high, second):
    core = here % 2
    step = low + (high - low) * (core + second - 2 * core * second)
    return [here ^ (k * step) for k in range(1, 4)]


def first_kernel(mine, got, order, *chip):
    new = mine[...] + got[...]
    for c in chip:
        c[...] = new


def middle_kernel(low, high, chip, *rest):
    *got, order, entered, m0, m1, m2 = rest
    here = lax.axis_index("seq")

    def rows(low_first):
        first = [here ^ (k * (low if low_first else high)) for k in range(1, 4)]
        second = [here ^ (k * (high if low_first else low)) for k in range(1, 4)]
        return first, second

    @pl.when(lax.rem(here, 2) == 0)
    def _():
        first, _ = rows(True)
        new = sum(g[...] * jnp.where(p < here, 1.0, 0.0) for g, p in zip(got, first))
        entered[...] = new
        total = chip[...] + got[0][...] + got[1][...] + got[2][...]
        for m in (m0, m1, m2):
            m[...] = total

    @pl.when(lax.rem(here, 2) == 1)
    def _():
        first, second = rows(False)
        new = sum(g[...] * jnp.where(p > here, 1.0, 0.0) for g, p in zip(got, first))
        entered[...] = new
        for m, p in zip((m0, m1, m2), second):
            m[...] = new + chip[...] * jnp.where(p < here, 1.0, 0.0)


def last_kernel(high, mine, before, *rest):
    *got, order, entered, message = rest
    here = lax.axis_index("seq")
    new = before[...]
    for k, g in enumerate(got):
        use = (lax.rem(here, 2) == 1) | ((here ^ ((k + 1) * high)) < here)
        new += g[...] * jnp.where(use, 1.0, 0.0)
    entered[...] = new
    message[...] = new + mine[...]


def inside_kernel(first, count, qs, ks, vs, gs, pt, sg, sgt, order, dq, dk, dv):
    at_row = lax.broadcasted_iota(jnp.int32, (CHUNK, CHUNK), 0)
    at_col = lax.broadcasted_iota(jnp.int32, (CHUNK, CHUNK), 1)
    upper = at_row <= at_col
    lower = at_row >= at_col
    work = [(n, h, which) for n in range(count) for h in range(HEADS) for which in range(3)]

    def load(n, h):
        tok = slice((first + n) * CHUNK, (first + n + 1) * CHUNK)
        return qs[h, n * CHUNK : (n + 1) * CHUNK, :], ks[h, tok, :], vs[h, tok, :], gs[h, tok, :]

    def score(n, h, which):
        qq, kk, vv, gg = load(n, h)
        a, b = ((gg, vv), (vv, gg), (kk, qq))[which]
        return halves(mm(a, stacked(b), ROWS))

    def finish(near, n, h, which):
        qq, kk, vv, gg = load(n, h)
        keep, left, right, state, out = (
            (lower, gg, kk, pt, dq),
            (upper, vv, qq, sgt, dk),
            (upper, kk, gg, sg, dv),
        )[which]
        hi, lo = parts(jnp.where(keep, near, 0.0))
        top = jnp.concatenate([hi, left[:, :HEAD]], axis=1)
        low = jnp.concatenate([lo, left[:, HEAD:]], axis=1)
        x = mm(jnp.concatenate([top, low], axis=0), jnp.concatenate([right, state[n, h]], axis=0))
        out[h, n * CHUNK : (n + 1) * CHUNK, :] = halves(x[:CHUNK]) + x[CHUNK:, :HEAD]

    ready = []
    for i in range(len(work) + LEAD):
        if i < len(work):
            ready.append(score(*work[i]))
        if i >= LEAD:
            finish(ready.pop(0), *work[i - LEAD])


def outside_kernel(ks, vs, gs, entered, got, *rest):
    partial = rest[: 3 * SLICES]
    outs = rest[3 * SLICES : 3 * SLICES + 3]
    obs = rest[3 * SLICES + 3 : -1]
    sems = rest[-1]
    sizes, firsts = cut_sizes(ks.shape[1] // CHUNK)
    pieces = piece_list(sizes)
    even = lax.rem(lax.axis_index("seq"), 2) == 0
    weights = []
    for h in range(HEADS):
        before = jnp.where(even, entered[h], got[h])
        after = jnp.where(even, got[h], entered[h])
        weights.append([twice(pair(w)) for w in (before, after.T, after)])

    def send(j, n):
        i, first, size = pieces[n]
        src = obs[i].at[j, pl.ds(first * CHUNK * HEADS, size * CHUNK * HEADS)]
        dst = outs[j].at[pl.ds((firsts[i] + first) * CHUNK * HEADS, size * CHUNK * HEADS)]
        return pltpu.make_async_copy(src, dst, sems.at[j, n])

    work = [(j, n) for j in range(3) for n in range(len(pieces))]
    for j, n in work:
        i, first, size = pieces[n]
        tile = size * CHUNK
        off = first * CHUNK
        base = firsts[i] * CHUNK + off
        for h in range(HEADS):
            x = halves(mm((gs, vs, ks)[j][h, base : base + tile, :], weights[h][j]))
            obs[i][j, pl.ds(off * HEADS + h, tile, HEADS), :] = x + partial[3 * i + j][h, off : off + tile, :]
        send(j, n).start()
    for j, n in work:
        send(j, n).wait()


VM = pl.BlockSpec(memory_space=pltpu.VMEM)
ANY = pl.BlockSpec(memory_space=pl.ANY)


def vmem(*arrays):
    return [pltpu.with_memory_space_constraint(a, pltpu.VMEM) for a in arrays]


def hbm(*arrays):
    return [pltpu.with_memory_space_constraint(a, pltpu.HBM) for a in arrays]


def body(sizes, queries, key_vectors, value_vectors, grad_output):
    tokens = queries.shape[0]
    chunks = tokens // CHUNK
    flat = [x.reshape(tokens * HEADS, HEAD) for x in (queries, key_vectors, value_vectors, grad_output)]

    tile = 512
    split_shape = pltpu.VMEM((HEADS, tokens, 2 * HEAD), BF16)
    cuts, firsts = cut_sizes(chunks)
    query_shapes = [pltpu.VMEM((HEADS, n * CHUNK, 2 * HEAD), BF16) for n in cuts]
    state_shapes = [pltpu.VMEM((n, HEADS, HEAD, 2 * HEAD), BF16) for n in cuts]
    own_shape = pltpu.VMEM((HEADS, HEAD, HEAD), F32)
    shapes = [split_shape] * 3 + [own_shape] * 2 + query_shapes + state_shapes * 3
    ks, vs, gs, mine, other, *kept = pl.pallas_call(
        functools.partial(states_kernel, tile),
        out_shape=shapes,
        in_specs=[ANY] * 4,
        out_specs=[VM] * len(shapes),
        scratch_shapes=[pltpu.VMEM((tokens // tile, tile * HEADS, HEAD), F32)] * 4
        + [pltpu.VMEM((2, HEADS, HEAD, HEAD), F32), pltpu.SemaphoreType.DMA((4, tokens // tile))],
        compiler_params=pltpu.CompilerParams(vmem_limit_bytes=20 * MIB),
        cost_estimate=pl.CostEstimate(flops=10**9, bytes_accessed=16 * MIB, transcendentals=0),
        name="states",
    )(*hbm(*flat))

    def small(kernel, name, outs, *args):
        return pl.pallas_call(
            kernel,
            out_shape=[own_shape] * outs,
            in_specs=[VM] * len(args),
            out_specs=[VM] * outs,
            compiler_params=pltpu.CompilerParams(vmem_limit_bytes=2 * MIB),
            cost_estimate=pl.CostEstimate(flops=10**5, bytes_accessed=MIB, transcendentals=0),
            name=name,
        )(*vmem(*args))

    partial = []

    def inside(order):
        at = len(partial) // 3
        n = cuts[at]
        made = pl.pallas_call(
            functools.partial(inside_kernel, firsts[at], n),
            out_shape=[pltpu.VMEM((HEADS, n * CHUNK, HEAD), F32)] * 3,
            in_specs=[VM] * 8,
            out_specs=[VM] * 3,
            compiler_params=pltpu.CompilerParams(vmem_limit_bytes=4 * MIB),
            cost_estimate=pl.CostEstimate(flops=n * 4 * 10**8, bytes_accessed=MIB, transcendentals=0),
            name="inside" + str(at),
        )(*vmem(kept[at], ks, vs, gs, *kept[SLICES + at :: SLICES], order))
        partial.extend(made)
        return made[0]

    devices = sizes["seq"]
    sibling = [(i, i ^ 1) for i in range(devices)]
    got = lax.ppermute(other, "seq", sibling)
    chips = small(first_kernel, "first", 3, mine, got, inside(other))

    side = math.isqrt(devices // 2)
    low, high = 2, 2 * side

    def swap(messages, second):
        out = []
        for k, m in enumerate(messages):
            pairs = [(d, partners(d, low, high, second)[k]) for d in range(devices)]
            out.append(lax.ppermute(m, "seq", pairs))
        return out

    got = swap(chips, 0)
    entered, *messages = small(functools.partial(middle_kernel, low, high), "middle", 4, chips[0], *got, inside(chips[0]))
    got = swap(messages, 1)
    kernel = functools.partial(last_kernel, high)
    entered, message = small(kernel, "last", 2, mine, entered, *got, inside(messages[0]))
    got = lax.ppermute(message, "seq", sibling)
    while len(partial) < 3 * SLICES:
        inside(message)

    out = pl.pallas_call(
        outside_kernel,
        out_shape=[pltpu.HBM((tokens * HEADS, HEAD), F32)] * 3,
        in_specs=[VM] * (5 + 3 * SLICES),
        out_specs=[ANY] * 3,
        scratch_shapes=[pltpu.VMEM((3, n * CHUNK * HEADS, HEAD), F32) for n in cuts]
        + [pltpu.SemaphoreType.DMA((3, len(piece_list(cuts))))],
        compiler_params=pltpu.CompilerParams(vmem_limit_bytes=14 * MIB),
        cost_estimate=pl.CostEstimate(flops=10**9, bytes_accessed=12 * MIB, transcendentals=0),
        name="outside",
    )(*vmem(ks, vs, gs, entered, got, *partial))
    return tuple(x.reshape(queries.shape) for x in out)


def solution(mesh):
    spec = P(("seqs", "seq"), None, None)
    return jax.shard_map(
        functools.partial(body, dict(mesh.shape)),
        mesh=mesh,
        in_specs=(spec,) * 4,
        out_specs=(spec,) * 3,
        check_vma=False,
    )
```
